32 devices in a mesh: orb: 8 (over z, y), rep: 4 (over x, core).
Axes of the slice: x: 2, y: 2, z: 4, core: 2. Of those that a mesh axis runs over, the one named last changes fastest.
Arguments:
- blocks: bfloat16 [16, 1024, 512], P('orb', 'rep'), may hold values from -1.078125 to 1.078125
- amplitudes: bfloat16 [64, 512, 512], P('orb', 'rep'), may hold values from -3 to 3
- pair_orbitals: int32 [64, 2], P('orb'), may hold values from 0 to 15, as said below
- coupling: int32 [64, 4], P('orb'), may hold values from 0 to 63, as said below
- fock_coupling: bfloat16 [64, 4], P('orb'), may hold values from -0.5 to 0.5
- virtual_energy: float32 [512], replicated, may hold values from 0.3 to 2
- occupied_energy: float32 [16], replicated, may hold values from -1.5 to -0.1
Outputs:
- updated_amplitudes: bfloat16 [64, 512, 512], P('orb', 'rep')
The draws below stay inside these ranges and needn't reach their ends.
Inputs may be any that keep to these rules, and one draw needn't show every extreme that they name: `pair_orbitals`: orbital o lives on owner o // 2 and pair p on owner p // 8. A pair's first orbital lies on the pair's owner; its second lies on the same owner or the next one. `coupling`: every coupled pair lies on the pair's owner or on an adjacent owner.
All inputs are finite; a program needn't handle non-finite values.
Results may differ from the reference program's by a relative error of at most 0.01.
Values may be sent and summed in bfloat16 or wider, within the bound.
A program may use at most 64 MiB of HBM per device.

```python
import math
import jax
import jax.numpy as jnp
from jax import lax

NAUX = 1024
NV = 512
NCPL = 4
ORB_DEV = 2
PAIR_DEV = 8
AUXQ = 256
NOCC = 16
NPAIR = 64


def draw_pair_orbitals(key, part):
    owner_total = NPAIR // PAIR_DEV
    first_key = jax.random.fold_in(key, 11)
    second_key = jax.random.fold_in(key, 12)
    offset_key = jax.random.fold_in(key, 13)
    pair_owner = jnp.arange(NPAIR, dtype=jnp.int32) // PAIR_DEV
    first_orbital = pair_owner * ORB_DEV + jax.random.randint(first_key, (NPAIR,), 0, ORB_DEV, dtype=jnp.int32)
    next_owner = jnp.minimum(pair_owner + jax.random.randint(offset_key, (NPAIR,), 0, 2, dtype=jnp.int32), owner_total - 1)
    second_orbital = next_owner * ORB_DEV + jax.random.randint(second_key, (NPAIR,), 0, ORB_DEV, dtype=jnp.int32)
    return jnp.stack([first_orbital, second_orbital], axis=1).astype(jnp.int32)


def draw_coupling(key, part):
    owner_total = NPAIR // PAIR_DEV
    offset_key = jax.random.fold_in(key, 21)
    slot_key = jax.random.fold_in(key, 22)
    pair_owner = (jnp.arange(NPAIR, dtype=jnp.int32) // PAIR_DEV)[:, None]
    offsets = jax.random.randint(offset_key, (NPAIR, NCPL), -1, 2, dtype=jnp.int32)
    target_owner = jnp.clip(pair_owner + offsets, 0, owner_total - 1)
    slots = jax.random.randint(slot_key, (NPAIR, NCPL), 0, PAIR_DEV, dtype=jnp.int32)
    return (target_owner * PAIR_DEV + slots).astype(jnp.int32)


def shard_levels(rng, extent, cuts, low, top_value):
    factor_of = 1.0
    for dim, parts in cuts:
        heights = jax.random.uniform(jax.random.fold_in(jax.random.fold_in(rng, 6), dim), (parts,), jnp.float32, low / len(cuts), top_value / len(cuts))
        factor_of = factor_of * jnp.repeat(jnp.exp(heights), extent[dim] // parts).reshape((-1,) + (1,) * (len(extent) - 1 - dim))
    return factor_of


def normal_values(rng, extent, scale, bound, cuts=(), kind=jnp.bfloat16):
    level = shard_levels(rng, extent, cuts, -0.22, 0.18) if cuts else 1.0
    values = jax.random.normal(rng, extent, jnp.float32) * scale * level
    return jnp.minimum(jnp.maximum(values, -bound), bound).astype(kind)


def setup_inputs(seed: int = 0) -> dict:
    arg_keys = jax.random.split(jax.random.key(seed), 8)
    return {
        "blocks": normal_values(arg_keys[0], (NOCC, NAUX, NV), 0.18, 1.078125, ((0, 8), (1, 4))),
        "amplitudes": normal_values(arg_keys[1], (NPAIR, NV, NV), 0.5, 3.0, ((0, 8), (1, 4))),
        "pair_orbitals": draw_pair_orbitals(jax.random.fold_in(arg_keys[7], 71), 0),
        "coupling": draw_coupling(jax.random.fold_in(arg_keys[7], 71), 0),
        "fock_coupling": jnp.clip(jax.random.uniform(arg_keys[4], (NPAIR, NCPL), jnp.float32, -0.5, 0.5) * shard_levels(arg_keys[4], (NPAIR, NCPL), ((0, 8),), -0.4, 0.0), -0.5, 0.5).astype(jnp.bfloat16),
        "virtual_energy": jnp.clip(jnp.exp(jax.random.uniform(arg_keys[5], (NV,), jnp.float32, math.log(0.3), math.log(2.0))), 0.3, 2.0),
        "occupied_energy": jnp.clip(jax.random.uniform(arg_keys[6], (NOCC,), jnp.float32, -1.5, -0.1), -1.5, -0.1),
    }


damping = 0.7


def reference(blocks, amplitudes, pair_orbitals, coupling, fock_coupling, virtual_energy, occupied_energy):
    def one_pair(pair_index):
        first_orbital = pair_orbitals[pair_index, 0]
        second_orbital = pair_orbitals[pair_index, 1]
        left_block = blocks[first_orbital].astype(jnp.float32).reshape(NAUX // AUXQ, AUXQ, NV)
        right_block = blocks[second_orbital].astype(jnp.float32).reshape(NAUX // AUXQ, AUXQ, NV)
        partial_value = jnp.einsum("gqa,gqb->gab", left_block, right_block, precision=lax.Precision.HIGHEST)
        rounded = lax.optimization_barrier(partial_value.astype(jnp.bfloat16))
        integrals = jnp.sum(rounded.astype(jnp.float32), axis=0)
        picked = amplitudes[coupling[pair_index]].astype(jnp.float32)
        weights = fock_coupling[pair_index].astype(jnp.float32)
        coupled = jnp.einsum("c,cab->ab", weights, picked, precision=lax.Precision.HIGHEST)
        pair_shift = occupied_energy[first_orbital] + occupied_energy[second_orbital]
        denominator = virtual_energy[:, None] + virtual_energy[None, :] - pair_shift
        previous = amplitudes[pair_index].astype(jnp.float32)
        updated = (1.0 - damping) * previous - damping * (integrals - coupled) / denominator
        return updated.astype(jnp.bfloat16)

    return lax.map(one_pair, jnp.arange(NPAIR, dtype=jnp.int32))
```

```python
import functools

import jax
import jax.numpy as jnp
from jax import lax
from jax.experimental import pallas as pl
from jax.experimental.pallas import tpu as pltpu
from jax.sharding import PartitionSpec as P

MESH = pl.DeviceIdType.MESH
damping = 0.7


def kernel(
    peers, groups, chunks,
    blocks, amps, pairs, coupling, fock, virtual, occupied,
    out,
    own, nxt, integrals, weights, column, result, *rest,
):
    parts = rest[:chunks]
    (own_sem, amp_sem, out_sem, nxt_send, nxt_recv, own_send, own_recv, far_send, far_recv,
     amp_send, amp_recv, fwd_send, fwd_recv) = rest[chunks:]
    orbitals, quarter, full = blocks.shape
    count, rows = amps.shape[:2]
    height = rows // chunks
    coupled_count = coupling.shape[1]
    o = lax.axis_index("orb")
    r = lax.axis_index("rep")
    even = lax.rem(o, 2) == 0
    has_prev, has_next = o > 0, o < peers - 1
    has_back2, has_on2 = o > 1, o < peers - 2
    partner = jnp.where(even, o + 1, o - 1)
    near_slot = jnp.where(even, 2 * count, 0)
    far_slot = jnp.where(even, 0, 2 * count)
    has_fwd = jnp.logical_or(jnp.logical_and(even, has_on2), jnp.logical_and(~even, has_back2))
    has_far = jnp.logical_or(jnp.logical_and(even, has_back2), jnp.logical_and(~even, has_on2))
    fwd_target = jnp.where(even, o + 2, o - 2)
    bits = [1 << b for b in reversed(range(groups.bit_length() - 1))]

    def remote(src, dst, send, recv, where):
        return pltpu.make_async_remote_copy(
            src_ref=src, dst_ref=dst, send_sem=send, recv_sem=recv, device_id=where, device_id_type=MESH
        )

    def flip(bit):
        return {"rep": jnp.where(lax.rem(r // bit, 2) == 0, r + bit, r - bit)}

    own_copy = pltpu.make_async_copy(blocks, own.at[0], own_sem)
    own_copy.start()
    amp_copies = [
        pltpu.make_async_copy(
            amps.at[:, pl.ds(k * height, height), :], parts[k].at[pl.ds(count, count)], amp_sem.at[k]
        )
        for k in range(chunks)
    ]
    for copy in amp_copies:
        copy.start()

    barrier = pltpu.get_barrier_semaphore()
    for bit in bits:
        pl.semaphore_signal(barrier, inc=1, device_id=flip(bit), device_id_type=MESH)
    for there, distance in ((has_prev, -1), (has_next, 1), (has_back2, -2), (has_on2, 2)):
        @pl.when(there)
        def _():
            pl.semaphore_signal(barrier, inc=1, device_id={"orb": o + distance}, device_id_type=MESH)
    ones = [jnp.where(there, 1, 0) for there in (has_prev, has_next, has_back2, has_on2)]
    pl.semaphore_wait(barrier, len(bits) + sum(ones))

    def block_copy(j):
        return remote(blocks.at[j], nxt.at[0, j], nxt_send.at[j], nxt_recv.at[j], {"orb": o - 1})

    def own_hop(m, bit, j):
        src = blocks.at[j] if m == 0 else own.at[m, j]
        return remote(src, own.at[m + bit, j], own_send.at[m + bit, j], own_recv.at[m + bit, j], flip(bit))

    def far_hop(m, bit, j):
        return remote(
            nxt.at[m, j], nxt.at[m + bit, j], far_send.at[m + bit, j], far_recv.at[m + bit, j], flip(bit)
        )

    def amp_copy(k):
        return remote(
            amps.at[:, pl.ds(k * height, height), :], parts[k].at[pl.ds(far_slot, count)],
            amp_send.at[k], amp_recv.at[k], {"orb": partner},
        )

    def amp_arrival(k):
        return remote(
            amps.at[:, pl.ds(k * height, height), :], parts[k].at[pl.ds(near_slot, count)],
            amp_send.at[k], amp_recv.at[k], {"orb": partner},
        )

    def fwd_copy(k):
        return remote(
            parts[k].at[pl.ds(near_slot, count)], parts[k].at[pl.ds(far_slot, count)],
            fwd_send.at[k], fwd_recv.at[k], {"orb": fwd_target},
        )

    hops, held = [], [0]
    for bit in bits:
        hops += [(m, bit) for m in held]
        held += [m + bit for m in held]

    @pl.when(has_prev)
    def _():
        for j in range(orbitals):
            block_copy(j).start()
    for m, bit in hops:
        if m == 0:
            for j in range(orbitals):
                own_hop(m, bit, j).start()
    for k in range(chunks):
        amp_copy(k).start()

    def forward(k):
        amp_arrival(k).wait_recv()

        @pl.when(has_fwd)
        def _():
            fwd_copy(k).start()

    @pl.when(has_next)
    def _():
        for j in range(orbitals):
            block_copy(j).wait_recv()
            for m, bit in hops:
                if m == 0:
                    far_hop(m, bit, j).start()

    weights[...] = fock[...].astype(jnp.float32)
    mine = virtual[:, pl.ds(pl.multiple_of(r * rows, rows), rows)]
    column[...] = jnp.transpose(jnp.broadcast_to(mine, (rows, rows)))
    own_copy.wait()
    arrivals = {m + bit: (m, bit) for m, bit in hops}
    later = {m: [(a, b) for a, b in hops if a == m] for m in range(1, groups)}

    def settle(hop, slot):
        m, bit = arrivals[slot]
        for j in range(orbitals):
            hop(m, bit, j).wait_recv()
            for a, b in later[slot]:
                hop(a, b, j).start()

    order = sorted(range(1, groups), key=lambda slot: [h for h in hops].index(arrivals[slot]))
    columns = pl.ds(pl.multiple_of(r * rows, rows), rows)

    def combos(right, i, shift):
        for j in range(orbitals):
            total = None
            for m in range(groups):
                product = lax.dot_general(
                    own[m, i, :, columns], right[m, j], (((0,), (0,)), ((), ())),
                    preferred_element_type=jnp.float32,
                )
                term = product.astype(jnp.bfloat16).astype(jnp.float32)
                total = term if total is None else total + term
            integrals[i * 2 * orbitals + shift + j] = total

    def far_slots():
        @pl.when(has_next)
        def _():
            for slot in order:
                settle(far_hop, slot)

    def far_combos(i):
        @pl.when(has_next)
        def _():
            combos(nxt, i, orbitals)

    for slot in order:
        settle(own_hop, slot)
    forward(0)
    for i in range(orbitals):
        combos(own, i, 0)
        forward(min(1 + i, chunks - 1)) if 1 + i < chunks else None
    sent = min(1 + orbitals, chunks)
    far_slots()
    for i in range(orbitals):
        if sent < chunks:
            forward(sent)
            sent += 1
        far_combos(i)

    base = o * orbitals
    first_pair = (o - 1) * count
    row = virtual[...]

    def finish(k):
        @pl.when(has_far)
        def _():
            fwd_copy(k).wait_recv()
        amp_copies[k].wait()
        spot = pl.ds(k * height, height)

        @pl.loop(0, count)
        def _(p):
            first, second = pairs[p, 0], pairs[p, 1]
            shift = occupied[first] + occupied[second]
            left, right = jnp.clip(first - base, 0, orbitals - 1), jnp.clip(second - base, 0, 2 * orbitals - 1)
            weight = weights[pl.ds(p, 1), :]
            coupled = None
            for c in range(coupled_count):
                place = jnp.clip(coupling[p, c] - first_pair, 0, 3 * count - 1)
                picked = parts[k][place].astype(jnp.float32)
                term = weight[:, c : c + 1] * picked
                coupled = term if coupled is None else coupled + term
            combo = left * 2 * orbitals + right
            residual = integrals[combo, spot, :] - coupled
            denominator = column[spot, 0:1] + row - shift
            previous = parts[k][count + p].astype(jnp.float32)
            updated = (1.0 - damping) * previous - damping * residual / denominator
            result[p, spot, :] = updated.astype(jnp.bfloat16)

        pltpu.make_async_copy(result.at[:, spot, :], out.at[:, spot, :], out_sem.at[k]).start()

    for k in range(chunks):
        while sent < min(chunks, k + 3):
            forward(sent)
            sent += 1
        finish(k)

    for k in range(chunks):
        spot = pl.ds(k * height, height)
        amp_copy(k).wait_send()
        pltpu.make_async_copy(result.at[:, spot, :], out.at[:, spot, :], out_sem.at[k]).wait()
    for m, bit in hops:
        for j in range(orbitals):
            own_hop(m, bit, j).wait_send()

    @pl.when(has_prev)
    def _():
        for j in range(orbitals):
            block_copy(j).wait_send()

    @pl.when(has_next)
    def _():
        for m, bit in hops:
            for j in range(orbitals):
                far_hop(m, bit, j).wait_send()

    @pl.when(has_fwd)
    def _():
        for k in range(chunks):
            fwd_copy(k).wait_send()


def solution(mesh):
    peers, groups = mesh.shape["orb"], mesh.shape["rep"]
    assert peers % 2 == 0 and groups & (groups - 1) == 0

    def per_device(blocks, amplitudes, pairs, coupling, fock, virtual, occupied):
        orbitals, quarter, full = blocks.shape
        count, rows, _ = amplitudes.shape
        chunks = rows // 16
        dma = pltpu.SemaphoreType.DMA
        vmem = pltpu.VMEM
        any_space = pl.BlockSpec(memory_space=pl.ANY)
        smem = pl.BlockSpec(memory_space=pltpu.SMEM)
        in_vmem = pl.BlockSpec(memory_space=pltpu.VMEM)
        return pl.pallas_call(
            functools.partial(kernel, peers, groups, chunks),
            out_shape=jax.ShapeDtypeStruct(amplitudes.shape, amplitudes.dtype),
            in_specs=[any_space, any_space, smem, smem, in_vmem, in_vmem, smem],
            out_specs=any_space,
            scratch_shapes=[
                vmem((groups, orbitals, quarter, full), jnp.bfloat16),
                vmem((groups, orbitals, quarter, full), jnp.bfloat16),
                vmem((2 * orbitals * orbitals, rows, full), jnp.float32),
                vmem(fock.shape, jnp.float32),
                vmem((rows, rows), jnp.float32),
                vmem((count, rows, full), jnp.bfloat16),
                *[vmem((3 * count, rows // chunks, full), jnp.bfloat16) for _ in range(chunks)],
                dma, dma((chunks,)), dma((chunks,)),
                dma((orbitals,)), dma((orbitals,)),
                dma((groups, orbitals)), dma((groups, orbitals)),
                dma((groups, orbitals)), dma((groups, orbitals)),
                dma((chunks,)), dma((chunks,)), dma((chunks,)), dma((chunks,)),
            ],
            compiler_params=pltpu.CompilerParams(
                collective_id=0, has_side_effects=True, vmem_limit_bytes=56 * 1024 * 1024
            ),
        )(blocks, amplitudes, pairs, coupling, fock, virtual.reshape(1, full), occupied)

    placed = (
        P("orb", "rep", None), P("orb", "rep", None), P("orb", None), P("orb", None), P("orb", None), P(), P(),
    )
    return jax.shard_map(
        per_device, mesh=mesh, in_specs=placed, out_specs=P("orb", "rep", None), check_vma=False
    )
```

```python
import functools

import jax
import jax.numpy as jnp
from jax import lax
from jax.experimental import pallas as pl
from jax.experimental.pallas import tpu as pltpu
from jax.sharding import PartitionSpec as P

MESH = pl.DeviceIdType.MESH
damping = 0.7
AHEAD = 1
HEIGHT = 16


def kernel(
    peers, groups, chunks,
    blocks, amps, pairs, coupling, fock, virtual, occupied,
    out,
    own, nxt, integrals, weights, column, result, *rest,
):
    parts = rest[:chunks]
    (own_sem, amp_sem, out_sem, nxt_send, nxt_recv, own_send, own_recv, far_send, far_recv,
     amp_send, amp_recv, fwd_send, fwd_recv) = rest[chunks:]
    orbitals, quarter, full = blocks.shape
    count, rows = amps.shape[:2]
    height = rows // chunks
    coupled_count = coupling.shape[0]
    o = lax.axis_index("orb")
    r = lax.axis_index("rep")
    even = lax.rem(o, 2) == 0
    has_prev, has_next = o > 0, o < peers - 1
    has_back2, has_on2 = o > 1, o < peers - 2
    partner = jnp.where(even, o + 1, o - 1)
    near_slot = jnp.where(even, 2 * count, 0)
    far_slot = jnp.where(even, 0, 2 * count)
    has_fwd = jnp.logical_or(jnp.logical_and(even, has_on2), jnp.logical_and(~even, has_back2))
    has_far = jnp.logical_or(jnp.logical_and(even, has_back2), jnp.logical_and(~even, has_on2))
    fwd_target = jnp.where(even, o + 2, o - 2)
    bits = [1 << b for b in reversed(range(groups.bit_length() - 1))]

    def remote(src, dst, send, recv, where):
        return pltpu.make_async_remote_copy(
            src_ref=src, dst_ref=dst, send_sem=send, recv_sem=recv, device_id=where, device_id_type=MESH
        )

    def flip(bit):
        return {"rep": jnp.where(lax.rem(r // bit, 2) == 0, r + bit, r - bit)}

    own_copy = pltpu.make_async_copy(blocks, own.at[0], own_sem)
    own_copy.start()
    amp_copies = [
        pltpu.make_async_copy(
            amps.at[:, pl.ds(k * height, height), :], parts[k].at[pl.ds(count, count)], amp_sem.at[k]
        )
        for k in range(chunks)
    ]
    for copy in amp_copies:
        copy.start()

    barrier = pltpu.get_barrier_semaphore()
    for bit in bits:
        pl.semaphore_signal(barrier, inc=1, device_id=flip(bit), device_id_type=MESH)
    for there, distance in ((has_prev, -1), (has_next, 1), (has_back2, -2), (has_on2, 2)):
        @pl.when(there)
        def _():
            pl.semaphore_signal(barrier, inc=1, device_id={"orb": o + distance}, device_id_type=MESH)
    ones = [jnp.where(there, 1, 0) for there in (has_prev, has_next, has_back2, has_on2)]
    pl.semaphore_wait(barrier, len(bits) + sum(ones))

    def block_copy(j):
        return remote(blocks.at[j], nxt.at[0, j], nxt_send.at[j], nxt_recv.at[j], {"orb": o - 1})

    def own_hop(m, bit, j):
        src = blocks.at[j] if m == 0 else own.at[m, j]
        return remote(src, own.at[m + bit, j], own_send.at[m + bit, j], own_recv.at[m + bit, j], flip(bit))

    def far_hop(m, bit, j):
        return remote(
            nxt.at[m, j], nxt.at[m + bit, j], far_send.at[m + bit, j], far_recv.at[m + bit, j], flip(bit)
        )

    def amp_copy(k):
        return remote(
            amps.at[:, pl.ds(k * height, height), :], parts[k].at[pl.ds(far_slot, count)],
            amp_send.at[k], amp_recv.at[k], {"orb": partner},
        )

    def amp_arrival(k):
        return remote(
            amps.at[:, pl.ds(k * height, height), :], parts[k].at[pl.ds(near_slot, count)],
            amp_send.at[k], amp_recv.at[k], {"orb": partner},
        )

    def fwd_copy(k):
        return remote(
            parts[k].at[pl.ds(near_slot, count)], parts[k].at[pl.ds(far_slot, count)],
            fwd_send.at[k], fwd_recv.at[k], {"orb": fwd_target},
        )

    hops, held = [], [0]
    for bit in bits:
        hops += [(m, bit) for m in held]
        held += [m + bit for m in held]

    @pl.when(has_prev)
    def _():
        for j in range(orbitals):
            block_copy(j).start()
    for m, bit in hops:
        if m == 0:
            for j in range(orbitals):
                own_hop(m, bit, j).start()
    issued = min(AHEAD, chunks)
    for k in range(issued):
        amp_copy(k).start()

    def forward(k):
        amp_arrival(k).wait_recv()

        @pl.when(has_fwd)
        def _():
            fwd_copy(k).start()

    for j in range(orbitals):
        @pl.when(has_prev)
        def _():
            block_copy(j).wait_send()
        upto = chunks if j == orbitals - 1 else min(issued + 1, chunks)
        for k in range(issued, upto):
            amp_copy(k).start()
        issued = upto

        @pl.when(has_next)
        def _():
            block_copy(j).wait_recv()
            for m, bit in hops:
                if m == 0:
                    far_hop(m, bit, j).start()

    weights[...] = jnp.transpose(fock[...].astype(jnp.float32))
    mine = virtual[:, pl.ds(pl.multiple_of(r * rows, rows), rows)]
    column[...] = jnp.transpose(jnp.broadcast_to(mine, (rows, rows)))
    own_copy.wait()
    arrivals = {m + bit: (m, bit) for m, bit in hops}
    later = {m: [(a, b) for a, b in hops if a == m] for m in range(1, groups)}

    def settle(hop, slot):
        m, bit = arrivals[slot]
        for j in range(orbitals):
            hop(m, bit, j).wait_recv()
            for a, b in later[slot]:
                hop(a, b, j).start()

    order = sorted(range(1, groups), key=lambda slot: [h for h in hops].index(arrivals[slot]))
    columns = pl.ds(pl.multiple_of(r * rows, rows), rows)

    def combos(right, i, shift):
        for j in range(orbitals):
            total = None
            for m in range(groups):
                product = lax.dot_general(
                    own[m, i, :, columns], right[m, j], (((0,), (0,)), ((), ())),
                    preferred_element_type=jnp.float32,
                )
                term = product.astype(jnp.bfloat16).astype(jnp.float32)
                total = term if total is None else total + term
            integrals[i * 2 * orbitals + shift + j] = total

    def far_slots():
        @pl.when(has_next)
        def _():
            for slot in order:
                settle(far_hop, slot)

    def far_combos(i):
        @pl.when(has_next)
        def _():
            combos(nxt, i, orbitals)

    settle(own_hop, order[0])
    forward(0)
    sent = 1
    for slot in order[1:]:
        settle(own_hop, slot)
    forward(1)
    sent = 2
    for i in range(orbitals):
        combos(own, i, 0)
        if sent < chunks:
            forward(sent)
            sent += 1
    while sent < chunks // 2:
        forward(sent)
        sent += 1
    far_slots()
    for i in range(orbitals):
        if sent < chunks:
            forward(sent)
            sent += 1
        far_combos(i)

    base = o * orbitals
    first_pair = (o - 1) * count
    row = virtual[...]

    def finish(k):
        @pl.when(has_far)
        def _():
            fwd_copy(k).wait_recv()
        amp_copies[k].wait()
        spot = pl.ds(k * height, height)

        @pl.loop(0, count, unroll=True)
        def _(p):
            first, second = pairs[0, p], pairs[1, p]
            shift = occupied[first] + occupied[second]
            left, right = jnp.clip(first - base, 0, orbitals - 1), jnp.clip(second - base, 0, 2 * orbitals - 1)
            weight = weights[pl.ds(p, 1), :]
            coupled = None
            for c in range(coupled_count):
                place = jnp.clip(coupling[c, p] - first_pair, 0, 3 * count - 1)
                picked = parts[k][place].astype(jnp.float32)
                term = weight[:, c : c + 1] * picked
                coupled = term if coupled is None else coupled + term
            combo = left * 2 * orbitals + right
            residual = integrals[combo, spot, :] - coupled
            denominator = column[spot, 0:1] + row - shift
            previous = parts[k][count + p].astype(jnp.float32)
            updated = (1.0 - damping) * previous - damping * residual / denominator
            result[p, spot, :] = updated.astype(jnp.bfloat16)

        pltpu.make_async_copy(result.at[:, spot, :], out.at[:, spot, :], out_sem.at[k]).start()

    for k in range(chunks):
        while sent < min(chunks, k + 3):
            forward(sent)
            sent += 1
        finish(k)

    for k in range(chunks):
        spot = pl.ds(k * height, height)
        amp_copy(k).wait_send()
        pltpu.make_async_copy(result.at[:, spot, :], out.at[:, spot, :], out_sem.at[k]).wait()
    for m, bit in hops:
        for j in range(orbitals):
            own_hop(m, bit, j).wait_send()

    @pl.when(has_next)
    def _():
        for m, bit in hops:
            for j in range(orbitals):
                far_hop(m, bit, j).wait_send()

    @pl.when(has_fwd)
    def _():
        for k in range(chunks):
            fwd_copy(k).wait_send()


def solution(mesh):
    peers, groups = mesh.shape["orb"], mesh.shape["rep"]
    assert peers % 2 == 0 and groups & (groups - 1) == 0

    def per_device(blocks, amplitudes, pairs, coupling, fock, virtual, occupied):
        orbitals, quarter, full = blocks.shape
        count, rows, _ = amplitudes.shape
        chunks = rows // HEIGHT
        dma = pltpu.SemaphoreType.DMA
        vmem = pltpu.VMEM
        any_space = pl.BlockSpec(memory_space=pl.ANY)
        smem = pl.BlockSpec(memory_space=pltpu.SMEM)
        in_vmem = pl.BlockSpec(memory_space=pltpu.VMEM)
        return pl.pallas_call(
            functools.partial(kernel, peers, groups, chunks),
            out_shape=jax.ShapeDtypeStruct(amplitudes.shape, amplitudes.dtype),
            in_specs=[any_space, any_space, smem, smem, in_vmem, in_vmem, smem],
            out_specs=any_space,
            scratch_shapes=[
                vmem((groups, orbitals, quarter, full), jnp.bfloat16),
                vmem((groups, orbitals, quarter, full), jnp.bfloat16),
                vmem((2 * orbitals * orbitals, rows, full), jnp.float32),
                vmem(fock.shape, jnp.float32),
                vmem((rows, rows), jnp.float32),
                vmem((count, rows, full), jnp.bfloat16),
                *[vmem((3 * count, rows // chunks, full), jnp.bfloat16) for _ in range(chunks)],
                dma, dma((chunks,)), dma((chunks,)),
                dma((orbitals,)), dma((orbitals,)),
                dma((groups, orbitals)), dma((groups, orbitals)),
                dma((groups, orbitals)), dma((groups, orbitals)),
                dma((chunks,)), dma((chunks,)), dma((chunks,)), dma((chunks,)),
            ],
            compiler_params=pltpu.CompilerParams(
                collective_id=0, has_side_effects=True, vmem_limit_bytes=56 * 1024 * 1024
            ),
        )(blocks, amplitudes, pairs.T, coupling.T, fock.T, virtual.reshape(1, full), occupied)

    placed = (
        P("orb", "rep", None), P("orb", "rep", None), P("orb", None), P("orb", None), P("orb", None), P(), P(),
    )
    return jax.shard_map(
        per_device, mesh=mesh, in_specs=placed, out_specs=P("orb", "rep", None), check_vma=False
    )
```

```python
import functools

import jax
import jax.numpy as jnp
from jax import lax
from jax.experimental import pallas as pl
from jax.experimental.pallas import tpu as pltpu
from jax.sharding import PartitionSpec as P

MESH = pl.DeviceIdType.MESH
damping = 0.7
AHEAD = 1
HEIGHT = 16


def kernel(
    peers, groups, chunks,
    blocks, amps, pairs, coupling, fock, virtual, occupied,
    out,
    own, nxt, integrals, weights, column, result, *rest,
):
    parts = rest[:chunks]
    (own_sem, amp_sem, out_sem, nxt_send, nxt_recv, own_send, own_recv, far_send, far_recv,
     amp_send, amp_recv, fwd_send, fwd_recv) = rest[chunks:]
    orbitals, quarter, full = blocks.shape
    count, rows = amps.shape[:2]
    height = rows // chunks
    coupled_count = coupling.shape[0]
    o = lax.axis_index("orb")
    r = lax.axis_index("rep")
    even = lax.rem(o, 2) == 0
    has_prev, has_next = o > 0, o < peers - 1
    has_back2, has_on2 = o > 1, o < peers - 2
    partner = jnp.where(even, o + 1, o - 1)
    near_slot = jnp.where(even, 2 * count, 0)
    far_slot = jnp.where(even, 0, 2 * count)
    has_fwd = jnp.logical_or(jnp.logical_and(even, has_on2), jnp.logical_and(~even, has_back2))
    has_far = jnp.logical_or(jnp.logical_and(even, has_back2), jnp.logical_and(~even, has_on2))
    fwd_target = jnp.where(even, o + 2, o - 2)
    bits = [1 << b for b in reversed(range(groups.bit_length() - 1))]

    def remote(src, dst, send, recv, where):
        return pltpu.make_async_remote_copy(
            src_ref=src, dst_ref=dst, send_sem=send, recv_sem=recv, device_id=where, device_id_type=MESH
        )

    def flip(bit):
        return {"rep": jnp.where(lax.rem(r // bit, 2) == 0, r + bit, r - bit)}

    own_copy = pltpu.make_async_copy(blocks, own.at[0], own_sem)
    own_copy.start()
    amp_copies = [
        pltpu.make_async_copy(
            amps.at[:, pl.ds(k * height, height), :], parts[k].at[pl.ds(count, count)], amp_sem.at[k]
        )
        for k in range(chunks)
    ]
    for copy in amp_copies:
        copy.start()

    barrier = pltpu.get_barrier_semaphore()
    for bit in bits:
        pl.semaphore_signal(barrier, inc=1, device_id=flip(bit), device_id_type=MESH)
    for there, distance in ((has_prev, -1), (has_next, 1), (has_back2, -2), (has_on2, 2)):
        @pl.when(there)
        def _():
            pl.semaphore_signal(barrier, inc=1, device_id={"orb": o + distance}, device_id_type=MESH)
    ones = [jnp.where(there, 1, 0) for there in (has_prev, has_next, has_back2, has_on2)]
    pl.semaphore_wait(barrier, len(bits) + sum(ones))

    def block_copy(j):
        return remote(blocks.at[j], nxt.at[0, j], nxt_send.at[j], nxt_recv.at[j], {"orb": o - 1})

    def own_hop(m, bit, j):
        src = blocks.at[j] if m == 0 else own.at[m, j]
        return remote(src, own.at[m + bit, j], own_send.at[m + bit, j], own_recv.at[m + bit, j], flip(bit))

    def far_hop(m, bit, j):
        return remote(
            nxt.at[m, j], nxt.at[m + bit, j], far_send.at[m + bit, j], far_recv.at[m + bit, j], flip(bit)
        )

    def amp_copy(k):
        return remote(
            amps.at[:, pl.ds(k * height, height), :], parts[k].at[pl.ds(far_slot, count)],
            amp_send.at[k], amp_recv.at[k], {"orb": partner},
        )

    def amp_arrival(k):
        return remote(
            amps.at[:, pl.ds(k * height, height), :], parts[k].at[pl.ds(near_slot, count)],
            amp_send.at[k], amp_recv.at[k], {"orb": partner},
        )

    def fwd_copy(k):
        return remote(
            parts[k].at[pl.ds(near_slot, count)], parts[k].at[pl.ds(far_slot, count)],
            fwd_send.at[k], fwd_recv.at[k], {"orb": fwd_target},
        )

    hops, held = [], [0]
    for bit in bits:
        hops += [(m, bit) for m in held]
        held += [m + bit for m in held]

    @pl.when(has_prev)
    def _():
        for j in range(orbitals):
            block_copy(j).start()
    issued = min(AHEAD, chunks)
    for k in range(issued):
        amp_copy(k).start()
    for m, bit in hops:
        if m == 0 and bit == bits[0]:
            for j in range(orbitals):
                own_hop(m, bit, j).start()

    def forward(k):
        amp_arrival(k).wait_recv()

        @pl.when(has_fwd)
        def _():
            fwd_copy(k).start()

    for j in range(orbitals):
        @pl.when(has_prev)
        def _():
            block_copy(j).wait_send()
        upto = chunks if j == orbitals - 1 else min(issued + 1, chunks)
        for k in range(issued, upto):
            amp_copy(k).start()
        issued = upto

        @pl.when(has_next)
        def _():
            block_copy(j).wait_recv()
            for m, bit in hops:
                if m == 0:
                    far_hop(m, bit, j).start()

    for m, bit in hops:
        if m == 0 and bit != bits[0]:
            for j in range(orbitals):
                own_hop(m, bit, j).start()
    weights[...] = jnp.transpose(fock[...].astype(jnp.float32))
    mine = virtual[:, pl.ds(pl.multiple_of(r * rows, rows), rows)]
    column[...] = jnp.transpose(jnp.broadcast_to(mine, (rows, rows)))
    own_copy.wait()
    arrivals = {m + bit: (m, bit) for m, bit in hops}
    later = {m: [(a, b) for a, b in hops if a == m] for m in range(1, groups)}

    def settle(hop, slot):
        m, bit = arrivals[slot]
        for j in range(orbitals):
            hop(m, bit, j).wait_recv()
            for a, b in later[slot]:
                hop(a, b, j).start()

    order = sorted(range(1, groups), key=lambda slot: [h for h in hops].index(arrivals[slot]))
    columns = pl.ds(pl.multiple_of(r * rows, rows), rows)

    def combos(right, i, shift):
        for j in range(orbitals):
            total = None
            for m in range(groups):
                product = lax.dot_general(
                    own[m, i, :, columns], right[m, j], (((0,), (0,)), ((), ())),
                    preferred_element_type=jnp.float32,
                )
                term = product.astype(jnp.bfloat16).astype(jnp.float32)
                total = term if total is None else total + term
            integrals[i * 2 * orbitals + shift + j] = total

    def far_slots():
        @pl.when(has_next)
        def _():
            for slot in order:
                settle(far_hop, slot)

    def far_combos(i):
        @pl.when(has_next)
        def _():
            combos(nxt, i, orbitals)

    forward(0)
    settle(own_hop, order[0])
    forward(1)
    for slot in order[1:]:
        settle(own_hop, slot)
    sent = 2
    for i in range(orbitals):
        combos(own, i, 0)
        if sent < chunks:
            forward(sent)
            sent += 1
    while sent < chunks // 2:
        forward(sent)
        sent += 1
    far_slots()
    for i in range(orbitals):
        if sent < chunks:
            forward(sent)
            sent += 1
        far_combos(i)

    base = o * orbitals
    first_pair = (o - 1) * count
    row = virtual[...]

    def finish(k):
        @pl.when(has_far)
        def _():
            fwd_copy(k).wait_recv()
        amp_copies[k].wait()
        spot = pl.ds(k * height, height)

        @pl.loop(0, count, unroll=True)
        def _(p):
            first, second = pairs[0, p], pairs[1, p]
            shift = occupied[first] + occupied[second]
            left, right = jnp.clip(first - base, 0, orbitals - 1), jnp.clip(second - base, 0, 2 * orbitals - 1)
            weight = weights[pl.ds(p, 1), :]
            coupled = None
            for c in range(coupled_count):
                place = jnp.clip(coupling[c, p] - first_pair, 0, 3 * count - 1)
                picked = parts[k][place].astype(jnp.float32)
                term = weight[:, c : c + 1] * picked
                coupled = term if coupled is None else coupled + term
            combo = left * 2 * orbitals + right
            residual = integrals[combo, spot, :] - coupled
            denominator = column[spot, 0:1] + row - shift
            previous = parts[k][count + p].astype(jnp.float32)
            updated = (1.0 - damping) * previous - damping * residual / denominator
            result[p, spot, :] = updated.astype(jnp.bfloat16)

        pltpu.make_async_copy(result.at[:, spot, :], out.at[:, spot, :], out_sem.at[k]).start()

    for k in range(chunks):
        while sent < min(chunks, k + 3):
            forward(sent)
            sent += 1
        finish(k)

    for k in range(chunks):
        spot = pl.ds(k * height, height)
        amp_copy(k).wait_send()
        pltpu.make_async_copy(result.at[:, spot, :], out.at[:, spot, :], out_sem.at[k]).wait()
    for m, bit in hops:
        for j in range(orbitals):
            own_hop(m, bit, j).wait_send()

    @pl.when(has_next)
    def _():
        for m, bit in hops:
            for j in range(orbitals):
                far_hop(m, bit, j).wait_send()

    @pl.when(has_fwd)
    def _():
        for k in range(chunks):
            fwd_copy(k).wait_send()


def solution(mesh):
    peers, groups = mesh.shape["orb"], mesh.shape["rep"]
    assert peers % 2 == 0 and groups & (groups - 1) == 0

    def per_device(blocks, amplitudes, pairs, coupling, fock, virtual, occupied):
        orbitals, quarter, full = blocks.shape
        count, rows, _ = amplitudes.shape
        chunks = rows // HEIGHT
        dma = pltpu.SemaphoreType.DMA
        vmem = pltpu.VMEM
        any_space = pl.BlockSpec(memory_space=pl.ANY)
        smem = pl.BlockSpec(memory_space=pltpu.SMEM)
        in_vmem = pl.BlockSpec(memory_space=pltpu.VMEM)
        return pl.pallas_call(
            functools.partial(kernel, peers, groups, chunks),
            out_shape=jax.ShapeDtypeStruct(amplitudes.shape, amplitudes.dtype),
            in_specs=[any_space, any_space, smem, smem, in_vmem, in_vmem, smem],
            out_specs=any_space,
            scratch_shapes=[
                vmem((groups, orbitals, quarter, full), jnp.bfloat16),
                vmem((groups, orbitals, quarter, full), jnp.bfloat16),
                vmem((2 * orbitals * orbitals, rows, full), jnp.float32),
                vmem(fock.shape, jnp.float32),
                vmem((rows, rows), jnp.float32),
                vmem((count, rows, full), jnp.bfloat16),
                *[vmem((3 * count, rows // chunks, full), jnp.bfloat16) for _ in range(chunks)],
                dma, dma((chunks,)), dma((chunks,)),
                dma((orbitals,)), dma((orbitals,)),
                dma((groups, orbitals)), dma((groups, orbitals)),
                dma((groups, orbitals)), dma((groups, orbitals)),
                dma((chunks,)), dma((chunks,)), dma((chunks,)), dma((chunks,)),
            ],
            compiler_params=pltpu.CompilerParams(
                collective_id=0, has_side_effects=True, vmem_limit_bytes=56 * 1024 * 1024
            ),
        )(blocks, amplitudes, pairs.T, coupling.T, fock.T, virtual.reshape(1, full), occupied)

    placed = (
        P("orb", "rep", None), P("orb", "rep", None), P("orb", None), P("orb", None), P("orb", None), P(), P(),
    )
    return jax.shard_map(
        per_device, mesh=mesh, in_specs=placed, out_specs=P("orb", "rep", None), check_vma=False
    )
```
